1024 devices in a mesh: dp: 8 (over z_lo, core), section: 16 (over z_hi, x), mp: 8 (over y).
Axes of the slice: x: 8, y: 8, z: 8 (z_hi: 2, z_lo: 4; z = z_hi * 4 + z_lo), core: 2. Of those that a mesh axis runs over, the one named last changes fastest.
Arguments:
- tokens: bfloat16 [4, 256, 4608], P(None, 'dp', 'mp'), may hold values from -6 to 6
- gain: float32 [16, 4608], P('section', 'mp'), may hold values from 0.1 to 1.9
- value_weight: bfloat16 [16, 4608, 2048], P('section', 'mp'), may hold values from -0.09375 to 0.09375
- out_weight: bfloat16 [16, 2048, 4608], P('section', None, 'mp'), may hold values from -0.125 to 0.125
- grad_prev: bfloat16 [8, 16, 1024, 4608], P('dp', 'section', None, 'mp'), may hold values from -18 to 18
- dither: bfloat16 [8, 16, 1024, 4608], P('dp', 'section', None, 'mp'), may hold values from 0 to 255, as said below
Outputs:
- hidden: float32 [16, 4, 256, 4608], P('section', None, 'dp', 'mp')
- grad_sum: bfloat16 [16, 1024, 4608], P('section', 'dp', 'mp')
- grad_scale: float32 [], replicated
The draws below stay inside these ranges and needn't reach their ends.
Inputs may be any that keep to these rules, and one draw needn't show every extreme that they name: `dither`: whole numbers.
All inputs are finite; a program needn't handle non-finite values. Where the reference program divides by a largest or mean magnitude, that divisor is 1e-20 or more.
Results may differ from the reference program's by a relative error of at most 0.04.
Values may be sent and summed in bfloat16 or wider, within the bound.
A program may use at most 32 MiB of HBM per device.

```python
import jax
import jax.numpy as jnp
from jax import lax

D = 4608
R = 2048
GR = 1024
MB = 4
BATCH = 256
N_DP = 8
N_SECTION = 16
N_MP = 8


def draw_grad_prev(key, part):
    key = jax.random.fold_in(key, 11)
    key_base, key_tail = jax.random.split(key)
    shape = (N_DP, N_SECTION, GR, D)
    base_values = jnp.clip(jax.random.normal(key_base, shape, jnp.float32), -6.0, 6.0)
    tail = jnp.exp(jax.random.uniform(key_tail, shape, jnp.float32, -4.0, 0.0))
    replica = jnp.arange(N_DP, dtype=jnp.float32)[:, None, None, None]
    section_pos = jnp.arange(N_SECTION, dtype=jnp.float32)[None, :, None, None]
    rise = 1.0 + 2.0 * (replica * N_SECTION + section_pos) / max(N_DP * N_SECTION - 1, 1)
    return (base_values * tail * rise).astype(jnp.bfloat16)


def draw_dither(key, part):
    key = jax.random.fold_in(key, 12)
    shape = (N_DP, N_SECTION, GR, D)
    uniform_values = jax.random.uniform(key, shape, jnp.float32, 0.0, 1.0)
    return jnp.clip(jnp.floor(uniform_values * 256.0), 0.0, 255.0).astype(jnp.bfloat16)


def level_of(rng, extent, pieces, low, top_value):
    factor_of, own = 1.0, jax.random.fold_in(rng, 6)
    for dim, blocks in pieces:
        draws = jnp.exp(jax.random.uniform(jax.random.fold_in(own, dim), (blocks,), jnp.float32, low / len(pieces), top_value / len(pieces)))
        factor_of = factor_of * jnp.repeat(draws, extent[dim] // blocks).reshape([-1 if axis == dim else 1 for axis in range(len(extent))])
    return factor_of


def noise(rng, shape, spread, bound, shards=(), kind=jnp.bfloat16):
    array = jax.random.normal(rng, shape, jnp.float32) * spread
    if len(shards) > 0:
        array = level_of(rng, shape, shards, -0.22, 0.18) * array
    return jnp.clip(array, min=-bound, max=bound).astype(kind)


def setup_inputs(seed: int = 0) -> dict:
    streams_of = jax.random.split(jax.random.key(seed), 7)
    tokens = noise(streams_of[0], (MB, BATCH, D), 1.0, 6.0, ((1, 8), (2, 8)))
    gain = jnp.clip(1.0 + 0.18 * jax.random.normal(streams_of[1], (N_SECTION, D), jnp.float32), 0.1, 1.9)
    value_weight = noise(streams_of[2], (N_SECTION, D, R), D ** -0.5, 0.09375, ((0, 16), (1, 8)))
    out_weight = noise(streams_of[3], (N_SECTION, R, D), R ** -0.5, 0.125, ((0, 16), (2, 8)))
    grad_prev = draw_grad_prev(jax.random.fold_in(streams_of[6], 71), 0)
    dither = draw_dither(jax.random.fold_in(streams_of[6], 71), 0)
    return {"tokens": tokens, "gain": gain, "value_weight": value_weight, "out_weight": out_weight, "grad_prev": grad_prev, "dither": dither}


def block_sum(terms):
    rounded = lax.optimization_barrier(terms.astype(jnp.bfloat16))
    return lax.optimization_barrier(jnp.sum(rounded.astype(jnp.float32), axis=0))

def section_layer(hidden_state, gain_row, weight_in, weight_out):
    row_count = hidden_state.shape[0]
    values = hidden_state
    scaled = (values * gain_row[None, :]).astype(jnp.bfloat16)
    scaled_blocks = scaled.reshape(row_count, N_MP, D // N_MP).astype(jnp.float32)
    weight_blocks = weight_in.reshape(N_MP, D // N_MP, R).astype(jnp.float32)
    partial_value = jnp.einsum('rkd,kdv->krv', scaled_blocks, weight_blocks)
    squares = lax.optimization_barrier(jnp.sum((values * values).reshape(row_count, N_MP, D // N_MP), axis=2)).T
    summed = block_sum(partial_value)
    square_sum = block_sum(squares)
    inverse = lax.rsqrt(square_sum / D + 1e-06)
    mixed_value = (summed * inverse[:, None]).astype(jnp.bfloat16)
    return values + jnp.dot(mixed_value, weight_out, preferred_element_type=jnp.float32)

def reference(tokens, gain, value_weight, out_weight, grad_prev, dither):
    hidden_state = tokens.reshape(MB * BATCH, D).astype(jnp.float32)
    outputs = []
    for section_id in range(N_SECTION):
        hidden_state = section_layer(hidden_state, gain[section_id].astype(jnp.float32), value_weight[section_id], out_weight[section_id])
        outputs.append(hidden_state.reshape(MB, BATCH, D))
    hidden = jnp.stack(outputs)
    peak_value = jnp.max(jnp.abs(grad_prev)).astype(jnp.float32)
    factor = 127.0 / peak_value

    def section_grad(section_id):
        grad_part = lax.dynamic_index_in_dim(grad_prev, section_id, 1, keepdims=False)
        level_part = lax.dynamic_index_in_dim(dither, section_id, 1, keepdims=False)
        shifted = grad_part.astype(jnp.float32) * factor + (level_part.astype(jnp.float32) + 0.5) / 256.0 - 0.5
        quantized = lax.optimization_barrier(jnp.clip(shifted, -127.0, 127.0).astype(jnp.bfloat16))
        return lax.optimization_barrier(jnp.sum(quantized.astype(jnp.float32), axis=0)).astype(jnp.bfloat16)
    grad_sum = lax.map(section_grad, jnp.arange(N_SECTION, dtype=jnp.int32))
    return (hidden, grad_sum, peak_value / 127.0)
```

```python
import functools

import jax
import jax.numpy as jnp
from jax import lax
from jax.experimental import pallas as pl
from jax.experimental.pallas import tpu as pltpu
from jax.sharding import PartitionSpec as P

MESH = pl.DeviceIdType.MESH
BF16, F32 = jnp.bfloat16, jnp.float32
CHUNK = 16
LAG_SUM = 2
LAG_OUT = 4


def wait_bytes(ref, sem):
    pltpu.make_async_copy(ref, ref, sem).wait()


def kernel(sizes, tokens, gain, w_value_hbm, w_out_hbm, grad_hbm, dither_hbm,
           hidden_out, sum_out, scale_out,
           w_value, w_own, w_prev, grad, levels,
           here, before, hidden, partial, parts, square, squares, value, gathered, gathered_own,
           quant, quants, peaks, peaks_dp, peaks_mp, peaks_sec,
           load_sem, part_s, part_r, square_s, square_r, value_s, value_r, own_r,
           ahead_s, before_r, back_s, hidden_r, ship_s, ship_r, twin_s, twin_r,
           quant_s, quant_r, peak_s, peak_r):
    n_dp, n_sec, n_mp = sizes
    chunks, rows, width = here.shape
    value_width = partial.shape[2]
    block = value_width // n_mp
    per_micro = tokens.shape[1] // rows
    half = w_prev.shape[0] // 2
    share = quant.shape[1]
    dp, sec, mp = (lax.axis_index(a) for a in ("dp", "section", "mp"))
    twin = dp + 1 - 2 * lax.rem(dp, 2)

    finishing = (0, n_sec // 2 - 1, n_sec - 1)

    def is_in(index, members):
        found = index == members[0]
        for member in members[1:]:
            found = jnp.logical_or(found, index == member)
        return found

    finishes = is_in(sec, finishing)
    hands_on = jnp.logical_not(finishes)
    takes_value = jnp.logical_and(sec > 0, jnp.logical_not(is_in(sec - 1, finishing)))
    takes_hidden = jnp.logical_and(sec > 0, is_in(sec - 1, finishing))
    first = sec == 0
    late = sec >= n_sec // 2

    def load(i, src, dst):
        return pltpu.make_async_copy(src, dst, load_sem.at[i])

    loads = [
        load(0, w_value_hbm.at[0], w_value),
        load(1, w_out_hbm.at[0], w_own),
        load(2, grad_hbm.at[0, 0], grad),
        load(3, dither_hbm.at[0, 0], levels),
    ]
    for item in loads:
        item.start()

    barrier = pltpu.get_barrier_semaphore()

    def greet(**where):
        pl.semaphore_signal(barrier, inc=1, device_id=where, device_id_type=MESH)

    for r in range(1, n_dp):
        greet(dp=lax.rem(dp + r, n_dp))
    for r in range(1, n_mp):
        greet(mp=lax.rem(mp + r, n_mp))
    for r in range(1, n_sec):
        greet(section=lax.rem(sec + r, n_sec))

    @pl.when(sec < n_sec - 1)
    def _():
        for r in range(1, n_mp):
            greet(section=sec + 1, mp=lax.rem(mp + r, n_mp))

    @pl.when(sec > 0)
    def _():
        for r in range(1, n_mp):
            greet(section=sec - 1, mp=lax.rem(mp + r, n_mp))

    sides = (sec > 0).astype(jnp.int32) + (sec < n_sec - 1).astype(jnp.int32)
    pl.semaphore_wait(barrier, n_dp + n_sec + n_mp - 3 + (n_mp - 1) * sides)

    def remote(src, dst, send, recv, **where):
        return pltpu.make_async_remote_copy(src, dst, send, recv, device_id=where, device_id_type=MESH)

    mine = pl.ds(pl.multiple_of(lax.rem(dp, 2) * half, half), half)
    other = pl.ds(pl.multiple_of(lax.rem(twin, 2) * half, half), half)

    @pl.when(hands_on)
    def _():
        remote(w_out_hbm.at[0, mine], w_prev.at[mine], ship_s, ship_r, section=sec + 1).start()

    def local_peak():
        loads[2].wait()

        def step(i, best):
            piece = grad[pl.ds(pl.multiple_of(i * 32, 32), 32), :].astype(F32)
            return jnp.maximum(best, jnp.abs(piece))

        best = lax.fori_loop(0, grad.shape[0] // 32, step, jnp.zeros((32, width), F32))
        best = jnp.max(jnp.max(best, axis=1, keepdims=True), axis=0, keepdims=True)
        peaks[0] = jnp.broadcast_to(best, (1, 128))

    def send_peak(stage, axis, size, index, dst):
        for r in range(1, size):
            remote(peaks.at[stage], dst.at[r - 1], peak_s.at[stage], peak_r.at[stage],
                   **{axis: lax.rem(index + r, size)}).start()

    def take_peak(stage, dst):
        wait_bytes(dst, peak_r.at[stage])
        peaks[stage + 1] = jnp.maximum(peaks[stage], jnp.max(dst[...], axis=0))

    def peak_a():
        local_peak()
        send_peak(0, "dp", n_dp, dp, peaks_dp)

    def peak_b():
        take_peak(0, peaks_dp)
        send_peak(1, "mp", n_mp, mp, peaks_mp)

    def peak_c():
        take_peak(1, peaks_mp)
        send_peak(2, "section", n_sec, sec, peaks_sec)

    def gradient():
        take_peak(2, peaks_sec)
        peak = peaks[3][:, :1]
        scale_out[...] = jnp.broadcast_to(peak / 127.0, scale_out.shape)
        factor = 127.0 / peak
        loads[3].wait()
        per = share // 32

        def step(i, carry):
            at = pl.ds(pl.multiple_of(i * 32, 32), 32)
            shifted = grad[at, :].astype(F32) * factor + (levels[at, :].astype(F32) + 0.5) / 256.0 - 0.5
            into = pl.ds(pl.multiple_of(lax.rem(i, per) * 32, 32), 32)
            quant[i // per, into, :] = jnp.clip(shifted, -127.0, 127.0).astype(BF16)
            return carry

        lax.fori_loop(0, n_dp * per, step, 0)
        for r in range(n_dp - 1, 0, -1):
            to = lax.rem(dp + r, n_dp)
            remote(quant.at[to], quants.at[r - 1], quant_s, quant_r, dp=to).start()
        wait_bytes(quants, quant_r)

        def add(i, carry):
            at = pl.ds(pl.multiple_of(i * 16, 16), 16)
            total = quant[dp, at, :].astype(F32)
            for r in range(n_dp - 1):
                total = total + quants[r, at, :].astype(F32)
            sum_out[0, at, :] = total.astype(BF16)
            return carry

        lax.fori_loop(0, share // 16, add, 0)

    @pl.when(jnp.logical_not(first))
    def _():
        peak_a()
        peak_b()
        peak_c()

    @pl.when(takes_value)
    def _():
        wait_bytes(w_prev.at[mine], ship_r)
        remote(w_prev.at[mine], w_prev.at[mine], twin_s, twin_r, dp=twin).start()

    @pl.when(late)
    def _():
        gradient()

    loads[0].wait()
    loads[1].wait()

    @pl.when(takes_value)
    def _():
        wait_bytes(w_prev.at[other], twin_r)

    diagonal = (lax.broadcasted_iota(jnp.int32, (rows, 128), 0)
                == lax.broadcasted_iota(jnp.int32, (rows, 128), 1))
    full_width = width * n_mp

    def project(c):
        @pl.when(first)
        def _():
            at = pl.ds(pl.multiple_of(lax.rem(c, per_micro) * rows, rows), rows)
            here[c] = tokens[c // per_micro, at, :].astype(F32)

        @pl.when(takes_hidden)
        def _():
            wait_bytes(before.at[c], before_r.at[c])
            here[c] = before[c]

        @pl.when(takes_value)
        def _():
            wait_bytes(before.at[c], before_r.at[c])
            wait_bytes(gathered.at[c], value_r.at[c])
            here[c] = before[c] + jnp.dot(gathered[c], w_prev[...], preferred_element_type=F32)

        state = here[c]
        summed = jnp.sum(state * state, axis=1, keepdims=True)
        square[c] = jnp.sum(jnp.where(diagonal, summed, 0.0), axis=0, keepdims=True)
        for r in (4, 3, 5, 2, 6, 1, 7):
            if r < n_mp:
                remote(square.at[c], squares.at[c, r - 1], square_s.at[c], square_r.at[c],
                       mp=lax.rem(mp + r, n_mp)).start()
        scaled = (state * gain[...]).astype(BF16)
        partial[c] = jnp.dot(scaled, w_value[...], preferred_element_type=F32).astype(BF16)
        for r in (4, 3, 5, 2, 6, 1, 7):
            if r < n_mp:
                to = lax.rem(mp + r, n_mp)
                columns = pl.ds(pl.multiple_of(to * block, block), block)
                remote(partial.at[c, :, columns], parts.at[c, r - 1], part_s.at[c], part_r.at[c], mp=to).start()

        @pl.when(hands_on)
        def _():
            remote(here.at[c], before.at[c], ahead_s.at[c], before_r.at[c], section=sec + 1).start()

        @pl.when(takes_value)
        def _():
            remote(here.at[c], hidden.at[c], back_s.at[c], hidden_r.at[c], section=sec - 1).start()

    def normalise(c):
        wait_bytes(squares.at[c], square_r.at[c])
        total_square = square[c]
        for r in range(n_mp - 1):
            total_square = total_square + squares[c, r]
        column = jnp.sum(jnp.where(diagonal, total_square, 0.0), axis=1, keepdims=True)
        inverse = lax.rsqrt(column / full_width + 1e-06)
        wait_bytes(parts.at[c], part_r.at[c])
        columns = pl.ds(pl.multiple_of(mp * block, block), block)
        total = partial[c, :, columns].astype(F32)
        for r in range(n_mp - 1):
            total = total + parts[c, r].astype(F32)
        value[c] = (total * inverse).astype(BF16)

        @pl.when(finishes)
        def _():
            for r in (4, 3, 5, 2, 6, 1, 7):
                if r < n_mp:
                    remote(value.at[c], gathered_own.at[c, :, columns], value_s.at[c], own_r.at[c],
                           mp=lax.rem(mp + r, n_mp)).start()
            pltpu.make_async_copy(value.at[c], gathered_own.at[c, :, columns], own_r.at[c]).start()

        @pl.when(hands_on)
        def _():
            for r in (4, 3, 5, 2, 6, 1, 7, 0):
                if r < n_mp:
                    remote(value.at[c], gathered.at[c, :, columns], value_s.at[c], value_r.at[c],
                           section=sec + 1, mp=lax.rem(mp + r, n_mp)).start()

    def finish(c):
        wait_bytes(gathered_own.at[c], own_r.at[c])
        hidden[c] = here[c] + jnp.dot(gathered_own[c], w_own[...], preferred_element_type=F32)

        @pl.when(sec < n_sec - 1)
        def _():
            remote(hidden.at[c], before.at[c], ahead_s.at[c], before_r.at[c], section=sec + 1).start()

    def within(c):
        return jnp.logical_and(c >= 0, c < chunks)

    def turn(i, carry):
        @pl.when(within(i))
        def _():
            project(i)

        @pl.when(jnp.logical_and(finishes, within(i - LAG_OUT)))
        def _():
            finish(i - LAG_OUT)

        @pl.when(within(i - LAG_SUM))
        def _():
            normalise(i - LAG_SUM)

        for k, stage in ((2, peak_a), (3, peak_b), (5, peak_c)):
            @pl.when(jnp.logical_and(first, i == k))
            def _(stage=stage):
                stage()

        return carry

    lax.fori_loop(0, chunks + LAG_OUT, turn, 0)

    @pl.when(jnp.logical_not(late))
    def _():
        gradient()

    def close(c, carry):
        wait_bytes(squares.at[c], square_s.at[c])
        wait_bytes(parts.at[c], part_s.at[c])

        @pl.when(finishes)
        def _():
            wait_bytes(gathered_own.at[c, :, pl.ds(0, value_width - block)], value_s.at[c])

        @pl.when(hands_on)
        def _():
            wait_bytes(gathered_own.at[c], value_s.at[c])
            wait_bytes(hidden.at[c], hidden_r.at[c])

        @pl.when(sec < n_sec - 1)
        def _():
            wait_bytes(here.at[c], ahead_s.at[c])

        @pl.when(takes_value)
        def _():
            wait_bytes(here.at[c], back_s.at[c])

        at = pl.ds(pl.multiple_of(lax.rem(c, per_micro) * rows, rows), rows)
        hidden_out[0, c // per_micro, at, :] = hidden[c]
        return carry

    lax.fori_loop(0, chunks, close, 0)
    wait_bytes(quants, quant_s)
    wait_bytes(peaks_dp, peak_s.at[0])
    wait_bytes(peaks_mp, peak_s.at[1])
    wait_bytes(peaks_sec, peak_s.at[2])

    @pl.when(hands_on)
    def _():
        wait_bytes(w_prev.at[mine], ship_s)

    @pl.when(takes_value)
    def _():
        wait_bytes(w_prev.at[mine], twin_s)


def solution(mesh):
    n_dp, n_sec, n_mp = (mesh.shape[a] for a in ("dp", "section", "mp"))

    def per_device(tokens, gain, w_value, w_out, grad_prev, dither):
        micro, batch, width = tokens.shape
        value_width = w_value.shape[2]
        grad_rows = grad_prev.shape[2]
        rows = CHUNK
        chunks = micro * batch // rows
        block = value_width // n_mp
        share = grad_rows // n_dp
        vmem, hbm = pl.BlockSpec(memory_space=pltpu.VMEM), pl.BlockSpec(memory_space=pl.ANY)
        dma = pltpu.SemaphoreType.DMA
        state = pltpu.VMEM((chunks, rows, width), F32)
        wide = pltpu.VMEM((chunks, rows, value_width), BF16)
        hidden, summed, scale = pl.pallas_call(
            functools.partial(kernel, (n_dp, n_sec, n_mp)),
            out_shape=(
                jax.ShapeDtypeStruct((1, micro, batch, width), F32),
                jax.ShapeDtypeStruct((1, share, width), BF16),
                jax.ShapeDtypeStruct((8, 128), F32),
            ),
            in_specs=[vmem, vmem, hbm, hbm, hbm, hbm],
            out_specs=(vmem, vmem, vmem),
            scratch_shapes=[
                pltpu.VMEM((width, value_width), BF16),
                pltpu.VMEM((value_width, width), BF16),
                pltpu.VMEM((value_width, width), BF16),
                pltpu.VMEM((grad_rows, width), BF16),
                pltpu.VMEM((grad_rows, width), BF16),
                state, state, state,
                wide,
                pltpu.VMEM((chunks, n_mp - 1, rows, block), BF16),
                pltpu.VMEM((chunks, 1, 128), F32),
                pltpu.VMEM((chunks, n_mp - 1, 1, 128), F32),
                pltpu.VMEM((chunks, rows, block), BF16),
                wide, wide,
                pltpu.VMEM((n_dp, share, width), BF16),
                pltpu.VMEM((n_dp - 1, share, width), BF16),
                pltpu.VMEM((4, 1, 128), F32),
                pltpu.VMEM((n_dp - 1, 1, 128), F32),
                pltpu.VMEM((n_mp - 1, 1, 128), F32),
                pltpu.VMEM((n_sec - 1, 1, 128), F32),
                dma((4,)),
                dma((chunks,)), dma((chunks,)), dma((chunks,)), dma((chunks,)),
                dma((chunks,)), dma((chunks,)), dma((chunks,)),
                dma((chunks,)), dma((chunks,)), dma((chunks,)), dma((chunks,)),
                dma, dma, dma, dma, dma, dma,
                dma((3,)), dma((3,)),
            ],
            compiler_params=pltpu.CompilerParams(
                collective_id=0, has_side_effects=True, vmem_limit_bytes=48 * 1024 * 1024
            ),
        )(tokens, gain, w_value, w_out, grad_prev, dither)
        return hidden, summed, scale[0, 0]

    return jax.shard_map(
        per_device,
        mesh=mesh,
        in_specs=(
            P(None, "dp", "mp"),
            P("section", "mp"),
            P("section", "mp", None),
            P("section", None, "mp"),
            P("dp", "section", None, "mp"),
            P("dp", "section", None, "mp"),
        ),
        out_specs=(P("section", None, "dp", "mp"), P("section", "dp", "mp"), P()),
        check_vma=False,
    )
```

```python
import functools

import jax
import jax.numpy as jnp
from jax import lax
from jax.experimental import pallas as pl
from jax.experimental.pallas import tpu as pltpu
from jax.sharding import PartitionSpec as P

MESH = pl.DeviceIdType.MESH
BF16, F32 = jnp.bfloat16, jnp.float32
CHUNK = 16
LAG_SUM = 1
LAG_OUT = 2


def far_first(n):
    return sorted(range(n), key=lambda r: (-min(r, n - r), r))


def wait_bytes(ref, sem):
    pltpu.make_async_copy(ref, ref, sem).wait()


def kernel(sizes, tokens, gain, w_value_hbm, w_out_hbm, grad_hbm, dither_hbm,
           hidden_out, sum_out, scale_out,
           w_value, w_own, w_prev, grad, levels,
           here, before, hidden, partial, parts, square, squares, value, gathered, gathered_own,
           quant, quants, peaks, peaks_dp, peaks_mp, peaks_sec, peaks_opposite,
           load_sem, part_s, part_r, square_s, square_r, value_s, value_r, own_r,
           ahead_s, before_r, back_s, hidden_r, ship_s, ship_r, twin_s, twin_r,
           quant_s, quant_r, peak_s, peak_r):
    n_dp, n_sec, n_mp = sizes
    chunks, rows, width = here.shape
    value_width = partial.shape[2]
    block = value_width // n_mp
    per_micro = tokens.shape[1] // rows
    half = w_prev.shape[0] // 2
    share = quant.shape[1]
    dp, sec, mp = (lax.axis_index(a) for a in ("dp", "section", "mp"))
    twin = dp + 1 - 2 * lax.rem(dp, 2)
    ring = n_sec // 2
    place = lax.rem(sec, ring)
    base = sec - place
    opposite = lax.rem(sec + ring, n_sec)

    finishing = (0, 1, n_sec // 2 - 1, n_sec - 1)

    def is_in(index, members):
        found = index == members[0]
        for member in members[1:]:
            found = jnp.logical_or(found, index == member)
        return found

    finishes = is_in(sec, finishing)
    hands_on = jnp.logical_not(finishes)
    takes_value = jnp.logical_and(sec > 0, jnp.logical_not(is_in(sec - 1, finishing)))
    takes_hidden = jnp.logical_and(sec > 0, is_in(sec - 1, finishing))
    first = sec == 0
    late = sec >= n_sec * 5 // 8

    out_order = far_first(n_mp)
    in_order = out_order[::-1]

    def block_at(i):
        return pl.ds(pl.multiple_of(i * block, block), block)

    def slot_of(origin):
        r = lax.rem(mp + n_mp - origin, n_mp)
        slot = 0
        for i, distance in enumerate(in_order):
            slot = jnp.where(r == distance, i, slot)
        return slot

    def load(i, src, dst):
        return pltpu.make_async_copy(src, dst, load_sem.at[i])

    for i, r in enumerate(out_order):
        load(0, w_value_hbm.at[0, :, block_at(lax.rem(mp + r, n_mp))], w_value.at[:, block_at(i)]).start()
    for i, r in enumerate(in_order):
        load(1, w_out_hbm.at[0, block_at(lax.rem(mp + n_mp - r, n_mp))], w_own.at[block_at(i)]).start()
    load(2, grad_hbm.at[0, 0], grad).start()
    load(3, dither_hbm.at[0, 0], levels).start()

    barrier = pltpu.get_barrier_semaphore()

    def greet(**where):
        pl.semaphore_signal(barrier, inc=1, device_id=where, device_id_type=MESH)

    for r in range(1, n_dp):
        greet(dp=lax.rem(dp + r, n_dp))
    for r in range(1, n_mp):
        greet(mp=lax.rem(mp + r, n_mp))
    for r in range(1, ring):
        greet(section=base + lax.rem(place + r, ring))
    greet(section=opposite)

    @pl.when(hands_on)
    def _():
        for r in range(1, n_mp):
            greet(section=sec + 1, mp=lax.rem(mp + r, n_mp))

    @pl.when(takes_value)
    def _():
        for r in range(1, n_mp):
            greet(section=sec - 1, mp=lax.rem(mp + r, n_mp))

    @pl.when(sec == ring - 1)
    def _():
        greet(section=sec + 1)

    @pl.when(sec == ring)
    def _():
        greet(section=sec - 1)

    sides = hands_on.astype(jnp.int32) + takes_value.astype(jnp.int32)
    middle = jnp.logical_or(sec == ring - 1, sec == ring).astype(jnp.int32)
    pl.semaphore_wait(barrier, n_dp + n_mp + ring - 2 + (n_mp - 1) * sides + middle)

    def remote(src, dst, send, recv, **where):
        return pltpu.make_async_remote_copy(src, dst, send, recv, device_id=where, device_id_type=MESH)

    half_blocks = n_mp // 2
    a_half = w_prev.at[pl.ds(0, half)]

    @pl.when(hands_on)
    def _():
        for i in range(half_blocks):
            origin = lax.rem(dp, 2) * half_blocks + i
            remote(w_out_hbm.at[0, block_at(origin)], w_prev.at[block_at(slot_of(origin))], ship_s, ship_r,
                   section=sec + 1).start()

    def local_peak():
        wait_bytes(grad, load_sem.at[2])

        def step(i, best):
            piece = grad[pl.ds(pl.multiple_of(i * 32, 32), 32), :].astype(F32)
            return jnp.maximum(best, jnp.abs(piece))

        best = lax.fori_loop(0, grad.shape[0] // 32, step, jnp.zeros((32, width), F32))
        best = jnp.max(jnp.max(best, axis=1, keepdims=True), axis=0, keepdims=True)
        peaks[0] = jnp.broadcast_to(best, (1, 128))

    def send_peak(stage, dst, others):
        for i, where in enumerate(others):
            remote(peaks.at[stage], dst.at[i], peak_s.at[stage], peak_r.at[stage], **where).start()

    def take_peak(stage, dst):
        wait_bytes(dst, peak_r.at[stage])
        peaks[stage + 1] = jnp.maximum(peaks[stage], jnp.max(dst[...], axis=0))

    def peak_a():
        local_peak()
        send_peak(0, peaks_dp, [dict(dp=lax.rem(dp + r, n_dp)) for r in range(1, n_dp)])

    def peak_b():
        take_peak(0, peaks_dp)
        send_peak(1, peaks_mp, [dict(mp=lax.rem(mp + r, n_mp)) for r in range(1, n_mp)])

    def peak_c():
        take_peak(1, peaks_mp)
        send_peak(2, peaks_opposite, [dict(section=opposite)])

    def peak_d():
        take_peak(2, peaks_opposite)
        send_peak(3, peaks_sec, [dict(section=base + lax.rem(place + r, ring)) for r in range(1, ring)])

    def gradient():
        take_peak(3, peaks_sec)
        peak = peaks[4][:, :1]
        scale_out[...] = jnp.broadcast_to(peak / 127.0, scale_out.shape)
        factor = 127.0 / peak
        wait_bytes(levels, load_sem.at[3])
        per = share // 32

        def step(i, carry):
            at = pl.ds(pl.multiple_of(i * 32, 32), 32)
            shifted = grad[at, :].astype(F32) * factor + (levels[at, :].astype(F32) + 0.5) / 256.0 - 0.5
            into = pl.ds(pl.multiple_of(lax.rem(i, per) * 32, 32), 32)
            quant[i // per, into, :] = jnp.clip(shifted, -127.0, 127.0).astype(BF16)
            return carry

        lax.fori_loop(0, n_dp * per, step, 0)
        for r in range(n_dp - 1, 0, -1):
            to = lax.rem(dp + r, n_dp)
            remote(quant.at[to], quants.at[r - 1], quant_s, quant_r, dp=to).start()
        wait_bytes(quants, quant_r)

        def add(i, carry):
            at = pl.ds(pl.multiple_of(i * 16, 16), 16)
            total = quant[dp, at, :].astype(F32)
            for r in range(n_dp - 1):
                total = total + quants[r, at, :].astype(F32)
            sum_out[0, at, :] = total.astype(BF16)
            return carry

        lax.fori_loop(0, share // 16, add, 0)

    @pl.when(jnp.logical_not(first))
    def _():
        peak_a()
        peak_b()
        peak_c()
        peak_d()

    @pl.when(takes_value)
    def _():
        wait_bytes(a_half, ship_r)
        for i in range(half_blocks):
            at = block_at(slot_of(lax.rem(dp, 2) * half_blocks + i))
            remote(w_prev.at[at], w_prev.at[at], twin_s, twin_r, dp=twin).start()

    @pl.when(late)
    def _():
        gradient()

    wait_bytes(w_value, load_sem.at[0])
    wait_bytes(w_own, load_sem.at[1])

    @pl.when(takes_value)
    def _():
        wait_bytes(a_half, twin_r)

    diagonal = (lax.broadcasted_iota(jnp.int32, (rows, 128), 0)
                == lax.broadcasted_iota(jnp.int32, (rows, 128), 1))
    full_width = width * n_mp

    near = (n_mp // 2 + 1) * block

    def mixed(c, blocks, sems, weight):
        wait_bytes(blocks.at[c, :, pl.ds(0, near)], sems.at[c, 0])
        wait_bytes(blocks.at[c, :, pl.ds(near, value_width - near)], sems.at[c, 1])
        return jnp.dot(blocks[c], weight[...], preferred_element_type=F32)

    def project(c):
        @pl.when(first)
        def _():
            at = pl.ds(pl.multiple_of(lax.rem(c, per_micro) * rows, rows), rows)
            here[c] = tokens[c // per_micro, at, :].astype(F32)

        @pl.when(takes_hidden)
        def _():
            wait_bytes(before.at[c], before_r.at[c])
            here[c] = before[c]

        @pl.when(takes_value)
        def _():
            wait_bytes(before.at[c], before_r.at[c])
            here[c] = before[c] + mixed(c, gathered, value_r, w_prev)

        state = here[c]
        summed = jnp.sum(state * state, axis=1, keepdims=True)
        square[c] = jnp.sum(jnp.where(diagonal, summed, 0.0), axis=0, keepdims=True)
        scaled = (state * gain[...]).astype(BF16)
        middle = value_width // 2
        for start in (0, middle):
            product = jnp.dot(scaled, w_value[:, start:start + middle], preferred_element_type=F32)
            partial[c, :, start:start + middle] = product.astype(BF16)
            for i, r in enumerate(out_order):
                if r > 0 and start <= i * block < start + middle:
                    to = lax.rem(mp + r, n_mp)
                    remote(partial.at[c, :, block_at(i)], parts.at[c, r - 1], part_s.at[c], part_r.at[c], mp=to).start()
                    remote(square.at[c], squares.at[c, r - 1], square_s.at[c], square_r.at[c], mp=to).start()

        @pl.when(hands_on)
        def _():
            remote(here.at[c], before.at[c], ahead_s.at[c], before_r.at[c], section=sec + 1).start()

        @pl.when(takes_value)
        def _():
            remote(here.at[c], hidden.at[c], back_s.at[c], hidden_r.at[c], section=sec - 1).start()

    def normalise(c):
        wait_bytes(squares.at[c], square_r.at[c])
        total_square = square[c]
        for r in range(n_mp - 1):
            total_square = total_square + squares[c, r]
        column = jnp.sum(jnp.where(diagonal, total_square, 0.0), axis=1, keepdims=True)
        inverse = lax.rsqrt(column / full_width + 1e-06)
        wait_bytes(parts.at[c], part_r.at[c])
        total = partial[c, :, value_width - block:].astype(F32)
        for r in range(n_mp - 1):
            total = total + parts[c, r].astype(F32)
        value[c] = (total * inverse).astype(BF16)

        def into(blocks, r):
            return blocks.at[c, :, block_at(in_order.index(r))]

        def group(r):
            return 0 if in_order.index(r) * block < near else 1

        @pl.when(finishes)
        def _():
            for r in out_order[:-1]:
                remote(value.at[c], into(gathered_own, r), value_s.at[c], own_r.at[c, group(r)],
                       mp=lax.rem(mp + r, n_mp)).start()
            pltpu.make_async_copy(value.at[c], into(gathered_own, 0), own_r.at[c, 0]).start()

        @pl.when(hands_on)
        def _():
            for r in out_order:
                remote(value.at[c], into(gathered, r), value_s.at[c], value_r.at[c, group(r)],
                       section=sec + 1, mp=lax.rem(mp + r, n_mp)).start()

    def finish(c):
        hidden[c] = here[c] + mixed(c, gathered_own, own_r, w_own)

        @pl.when(sec < n_sec - 1)
        def _():
            remote(hidden.at[c], before.at[c], ahead_s.at[c], before_r.at[c], section=sec + 1).start()

    def within(c):
        return jnp.logical_and(c >= 0, c < chunks)

    def turn(i, carry):
        @pl.when(within(i))
        def _():
            project(i)

        @pl.when(within(i - LAG_SUM))
        def _():
            normalise(i - LAG_SUM)

        @pl.when(jnp.logical_and(finishes, within(i - LAG_OUT)))
        def _():
            finish(i - LAG_OUT)

        return carry

    lax.fori_loop(0, chunks + LAG_OUT, turn, 0)

    @pl.when(first)
    def _():
        peak_a()
        peak_b()
        peak_c()
        peak_d()

    @pl.when(jnp.logical_not(late))
    def _():
        gradient()

    def close(c, carry):
        wait_bytes(squares.at[c], square_s.at[c])
        wait_bytes(parts.at[c], part_s.at[c])

        @pl.when(finishes)
        def _():
            wait_bytes(gathered_own.at[c, :, pl.ds(0, value_width - block)], value_s.at[c])

        @pl.when(hands_on)
        def _():
            wait_bytes(gathered_own.at[c], value_s.at[c])
            wait_bytes(hidden.at[c], hidden_r.at[c])

        @pl.when(sec < n_sec - 1)
        def _():
            wait_bytes(here.at[c], ahead_s.at[c])

        @pl.when(takes_value)
        def _():
            wait_bytes(here.at[c], back_s.at[c])

        at = pl.ds(pl.multiple_of(lax.rem(c, per_micro) * rows, rows), rows)
        hidden_out[0, c // per_micro, at, :] = hidden[c]
        return carry

    lax.fori_loop(0, chunks, close, 0)
    wait_bytes(quants, quant_s)
    wait_bytes(peaks_dp, peak_s.at[0])
    wait_bytes(peaks_mp, peak_s.at[1])
    wait_bytes(peaks_opposite, peak_s.at[2])
    wait_bytes(peaks_sec, peak_s.at[3])

    @pl.when(hands_on)
    def _():
        wait_bytes(a_half, ship_s)

    @pl.when(takes_value)
    def _():
        wait_bytes(a_half, twin_s)


def solution(mesh):
    n_dp, n_sec, n_mp = (mesh.shape[a] for a in ("dp", "section", "mp"))

    def per_device(tokens, gain, w_value, w_out, grad_prev, dither):
        micro, batch, width = tokens.shape
        value_width = w_value.shape[2]
        grad_rows = grad_prev.shape[2]
        rows = CHUNK
        chunks = micro * batch // rows
        block = value_width // n_mp
        share = grad_rows // n_dp
        vmem, hbm = pl.BlockSpec(memory_space=pltpu.VMEM), pl.BlockSpec(memory_space=pl.ANY)
        dma = pltpu.SemaphoreType.DMA
        state = pltpu.VMEM((chunks, rows, width), F32)
        wide = pltpu.VMEM((chunks, rows, value_width), BF16)
        hidden, summed, scale = pl.pallas_call(
            functools.partial(kernel, (n_dp, n_sec, n_mp)),
            out_shape=(
                jax.ShapeDtypeStruct((1, micro, batch, width), F32),
                jax.ShapeDtypeStruct((1, share, width), BF16),
                jax.ShapeDtypeStruct((8, 128), F32),
            ),
            in_specs=[vmem, vmem, hbm, hbm, hbm, hbm],
            out_specs=(vmem, vmem, vmem),
            scratch_shapes=[
                pltpu.VMEM((width, value_width), BF16),
                pltpu.VMEM((value_width, width), BF16),
                pltpu.VMEM((value_width, width), BF16),
                pltpu.VMEM((grad_rows, width), BF16),
                pltpu.VMEM((grad_rows, width), BF16),
                state, state, state,
                wide,
                pltpu.VMEM((chunks, n_mp - 1, rows, block), BF16),
                pltpu.VMEM((chunks, 1, 128), F32),
                pltpu.VMEM((chunks, n_mp - 1, 1, 128), F32),
                pltpu.VMEM((chunks, rows, block), BF16),
                wide, wide,
                pltpu.VMEM((n_dp, share, width), BF16),
                pltpu.VMEM((n_dp - 1, share, width), BF16),
                pltpu.VMEM((5, 1, 128), F32),
                pltpu.VMEM((n_dp - 1, 1, 128), F32),
                pltpu.VMEM((n_mp - 1, 1, 128), F32),
                pltpu.VMEM((n_sec // 2 - 1, 1, 128), F32),
                pltpu.VMEM((1, 1, 128), F32),
                dma((4,)),
                dma((chunks,)), dma((chunks,)), dma((chunks,)), dma((chunks,)),
                dma((chunks,)), dma((chunks, 2)), dma((chunks, 2)),
                dma((chunks,)), dma((chunks,)), dma((chunks,)), dma((chunks,)),
                dma, dma, dma, dma, dma, dma,
                dma((4,)), dma((4,)),
            ],
            compiler_params=pltpu.CompilerParams(
                collective_id=0, has_side_effects=True, vmem_limit_bytes=48 * 1024 * 1024
            ),
        )(tokens, gain, w_value, w_out, grad_prev, dither)
        return hidden, summed, scale[0, 0]

    return jax.shard_map(
        per_device,
        mesh=mesh,
        in_specs=(
            P(None, "dp", "mp"),
            P("section", "mp"),
            P("section", "mp", None),
            P("section", None, "mp"),
            P("dp", "section", None, "mp"),
            P("dp", "section", None, "mp"),
        ),
        out_specs=(P("section", None, "dp", "mp"), P("section", "dp", "mp"), P()),
        check_vma=False,
    )
```

```python
import functools

import jax
import jax.numpy as jnp
from jax import lax
from jax.experimental import pallas as pl
from jax.experimental.pallas import tpu as pltpu
from jax.sharding import PartitionSpec as P

MESH = pl.DeviceIdType.MESH
BF16, F32 = jnp.bfloat16, jnp.float32
CHUNK = 16
LAG_SUM = 1
LAG_OUT = 2


def far_first(n):
    return sorted(range(n), key=lambda r: (-min(r, n - r), r))


def wait_bytes(ref, sem):
    pltpu.make_async_copy(ref, ref, sem).wait()


def kernel(sizes, tokens, gain, w_value_hbm, w_out_hbm, grad_hbm, dither_hbm,
           hidden_out, sum_out, scale_out,
           w_value, w_own, w_prev, w_own_t, w_prev_t, grad, levels,
           here, before, hidden, partial, parts, square, squares, value, gathered, gathered_own,
           quant, quants, peaks, peaks_dp, peaks_mp, peaks_sec, peaks_opposite,
           load_sem, part_s, part_r, square_s, square_r, value_s, value_r, own_r,
           ahead_s, before_r, back_s, hidden_r, ship_s, ship_r, twin_s, twin_r,
           quant_s, quant_r, peak_s, peak_r):
    n_dp, n_sec, n_mp = sizes
    chunks, rows, width = here.shape
    value_width = partial.shape[2]
    block = value_width // n_mp
    per_micro = tokens.shape[1] // rows
    half = value_width // 2
    share = quant.shape[2]
    dp, sec, mp = (lax.axis_index(a) for a in ("dp", "section", "mp"))
    twin = dp + 1 - 2 * lax.rem(dp, 2)
    ring = n_sec // 2
    place = lax.rem(sec, ring)
    base = sec - place
    opposite = lax.rem(sec + ring, n_sec)

    finishing = (0, 1, n_sec // 2 - 1, n_sec - 1)

    def is_in(index, members):
        found = index == members[0]
        for member in members[1:]:
            found = jnp.logical_or(found, index == member)
        return found

    finishes = is_in(sec, finishing)
    hands_on = jnp.logical_not(finishes)
    takes_value = jnp.logical_and(sec > 0, jnp.logical_not(is_in(sec - 1, finishing)))
    takes_hidden = jnp.logical_and(sec > 0, is_in(sec - 1, finishing))
    first = sec == 0
    late = sec >= n_sec * 5 // 8

    out_order = far_first(n_mp)
    in_order = out_order[::-1]

    def block_at(i):
        return pl.ds(pl.multiple_of(i * block, block), block)

    def slot_of(origin):
        r = lax.rem(mp + n_mp - origin, n_mp)
        slot = 0
        for i, distance in enumerate(in_order):
            slot = jnp.where(r == distance, i, slot)
        return slot

    def load(i, src, dst):
        return pltpu.make_async_copy(src, dst, load_sem.at[i])

    for i, r in enumerate(out_order):
        load(0, w_value_hbm.at[0, :, block_at(lax.rem(mp + r, n_mp))], w_value.at[:, block_at(i)]).start()
    for i, r in enumerate(in_order):
        load(1, w_out_hbm.at[0, :, block_at(lax.rem(mp + n_mp - r, n_mp))], w_own.at[:, block_at(i)]).start()
    load(2, grad_hbm.at[0, 0], grad).start()
    load(3, dither_hbm.at[0, 0], levels).start()

    barrier = pltpu.get_barrier_semaphore()

    def greet(**where):
        pl.semaphore_signal(barrier, inc=1, device_id=where, device_id_type=MESH)

    for r in range(1, n_dp):
        greet(dp=lax.rem(dp + r, n_dp))
    for r in range(1, n_mp):
        greet(mp=lax.rem(mp + r, n_mp))
    for r in range(1, ring):
        greet(section=base + lax.rem(place + r, ring))
    greet(section=opposite)

    @pl.when(hands_on)
    def _():
        for r in range(1, n_mp):
            greet(section=sec + 1, mp=lax.rem(mp + r, n_mp))

    @pl.when(takes_value)
    def _():
        for r in range(1, n_mp):
            greet(section=sec - 1, mp=lax.rem(mp + r, n_mp))

    @pl.when(sec == ring - 1)
    def _():
        greet(section=sec + 1)

    @pl.when(sec == ring)
    def _():
        greet(section=sec - 1)

    sides = hands_on.astype(jnp.int32) + takes_value.astype(jnp.int32)
    middle = jnp.logical_or(sec == ring - 1, sec == ring).astype(jnp.int32)
    pl.semaphore_wait(barrier, n_dp + n_mp + ring - 2 + (n_mp - 1) * sides + middle)

    next_sec = sec + 1
    ring_mp = [lax.rem(mp + r, n_mp) for r in range(n_mp)]

    def remote(src, dst, send, recv, **where):
        where = {"dp": dp, "section": sec, "mp": mp, **where}
        return pltpu.make_async_remote_copy(src, dst, send, recv, device_id=where, device_id_type=MESH)

    half_blocks = n_mp // 2
    a_half = w_prev.at[:, pl.ds(0, half)]

    @pl.when(hands_on)
    def _():
        for i in range(half_blocks):
            origin = lax.rem(dp, 2) * half_blocks + i
            remote(w_out_hbm.at[0, :, block_at(origin)], w_prev.at[:, block_at(slot_of(origin))], ship_s, ship_r,
                   section=sec + 1).start()

    def local_peak():
        wait_bytes(grad, load_sem.at[2])

        def step(i, best):
            piece = grad[pl.ds(pl.multiple_of(i * 32, 32), 32), :].astype(F32)
            return jnp.maximum(best, jnp.abs(piece))

        best = lax.fori_loop(0, grad.shape[0] // 32, step, jnp.zeros((32, grad.shape[1]), F32))
        best = jnp.max(jnp.max(best, axis=1, keepdims=True), axis=0, keepdims=True)
        peaks[0] = jnp.broadcast_to(best, (1, 128))

    def send_peak(stage, dst, others):
        for i, where in enumerate(others):
            remote(peaks.at[stage], dst.at[i], peak_s.at[stage], peak_r.at[stage], **where).start()

    def take_peak(stage, dst):
        wait_bytes(dst, peak_r.at[stage])
        peaks[stage + 1] = jnp.maximum(peaks[stage], jnp.max(dst[...], axis=0))

    def peak_a():
        local_peak()
        send_peak(0, peaks_dp, [dict(dp=lax.rem(dp + r, n_dp)) for r in range(1, n_dp)])

    def peak_b():
        take_peak(0, peaks_dp)
        send_peak(1, peaks_mp, [dict(mp=lax.rem(mp + r, n_mp)) for r in range(1, n_mp)])

    def peak_c():
        take_peak(1, peaks_mp)
        send_peak(2, peaks_opposite, [dict(section=opposite)])

    def peak_d():
        take_peak(2, peaks_opposite)
        send_peak(3, peaks_sec, [dict(section=base + lax.rem(place + r, ring)) for r in range(1, ring)])

    def gradient():
        take_peak(3, peaks_sec)
        peak = peaks[4][:, :1]
        scale_out[...] = jnp.broadcast_to(peak / 127.0, scale_out.shape)
        factor = 127.0 / peak
        wait_bytes(levels, load_sem.at[3])

        def step(i, carry):
            at = pl.ds(pl.multiple_of(i * 32, 32), 32)
            shifted = grad[at, :].astype(F32) * factor + (levels[at, :].astype(F32) + 0.5) / 256.0 - 0.5
            rounded = jnp.clip(shifted, -127.0, 127.0).astype(BF16)
            for j in range(n_dp):
                quant[j, at, :] = rounded[:, j * share:(j + 1) * share]
            return carry

        lax.fori_loop(0, width // 32, step, 0)
        for r in range(n_dp - 1, 0, -1):
            to = lax.rem(dp + r, n_dp)
            remote(quant.at[to], quants.at[r - 1], quant_s, quant_r, dp=to).start()
        wait_bytes(quants, quant_r)

        def add(i, carry):
            at = pl.ds(pl.multiple_of(i * 16, 16), 16)
            total = quant[dp, at, :].astype(F32)
            for r in range(n_dp - 1):
                total = total + quants[r, at, :].astype(F32)
            sum_out[0, at, :] = total.astype(BF16)
            return carry

        lax.fori_loop(0, width // 16, add, 0)

    @pl.when(jnp.logical_not(first))
    def _():
        peak_a()
        peak_b()
        peak_c()
        peak_d()

    @pl.when(takes_value)
    def _():
        wait_bytes(a_half, ship_r)
        for i in range(half_blocks):
            at = block_at(slot_of(lax.rem(dp, 2) * half_blocks + i))
            remote(w_prev.at[:, at], w_prev.at[:, at], twin_s, twin_r, dp=twin).start()

    @pl.when(late)
    def _():
        gradient()

    def turned(src, dst):
        def step(i, carry):
            at = block_at(i)
            dst[at, :] = src[:, at].T
            return carry

        lax.fori_loop(0, n_mp, step, 0)

    wait_bytes(w_value, load_sem.at[0])
    wait_bytes(w_own, load_sem.at[1])

    @pl.when(jnp.logical_and(finishes, jnp.logical_not(first)))
    def _():
        turned(w_own, w_own_t)

    @pl.when(takes_value)
    def _():
        wait_bytes(a_half, twin_r)
        turned(w_prev, w_prev_t)

    diagonal = (lax.broadcasted_iota(jnp.int32, (rows, 128), 0)
                == lax.broadcasted_iota(jnp.int32, (rows, 128), 1))
    full_width = width * n_mp

    near = (n_mp // 2 + 1) * block

    def mixed(c, blocks, sems, weight, contracted=0):
        wait_bytes(blocks.at[c, :, pl.ds(0, near)], sems.at[c, 0])
        wait_bytes(blocks.at[c, :, pl.ds(near, value_width - near)], sems.at[c, 1])
        return lax.dot_general(blocks[c], weight[...], (((1,), (contracted,)), ((), ())), preferred_element_type=F32)

    def project(c):
        @pl.when(first)
        def _():
            at = pl.ds(pl.multiple_of(lax.rem(c, per_micro) * rows, rows), rows)
            here[c] = tokens[c // per_micro, at, :].astype(F32)

        @pl.when(takes_hidden)
        def _():
            wait_bytes(before.at[c], before_r.at[c])
            here[c] = before[c]

        @pl.when(takes_value)
        def _():
            wait_bytes(before.at[c], before_r.at[c])
            here[c] = before[c] + mixed(c, gathered, value_r, w_prev_t)

        state = here[c]
        summed = jnp.sum(state * state, axis=1, keepdims=True)
        square[c] = jnp.sum(jnp.where(diagonal, summed, 0.0), axis=0, keepdims=True)
        scaled = (state * gain[...]).astype(BF16)
        middle = value_width // 2
        for start in (0, middle):
            product = jnp.dot(scaled, w_value[:, start:start + middle], preferred_element_type=F32)
            partial[c, :, start:start + middle] = product.astype(BF16)
            for i, r in enumerate(out_order):
                if r > 0 and start <= i * block < start + middle:
                    to = ring_mp[r]
                    columns = pl.ds(i * block, block)
                    remote(partial.at[c, :, columns], parts.at[c, r - 1], part_s.at[c], part_r.at[c], mp=to).start()
                    remote(square.at[c], squares.at[c, r - 1], square_s.at[c], square_r.at[c], mp=to).start()

        @pl.when(hands_on)
        def _():
            remote(here.at[c], before.at[c], ahead_s.at[c], before_r.at[c], section=sec + 1).start()

        @pl.when(takes_value)
        def _():
            remote(here.at[c], hidden.at[c], back_s.at[c], hidden_r.at[c], section=sec - 1).start()

    def normalise(c):
        wait_bytes(squares.at[c], square_r.at[c])
        total_square = square[c]
        for r in range(n_mp - 1):
            total_square = total_square + squares[c, r]
        column = jnp.sum(jnp.where(diagonal, total_square, 0.0), axis=1, keepdims=True)
        inverse = lax.rsqrt(column / full_width + 1e-06)
        wait_bytes(parts.at[c], part_r.at[c])
        total = partial[c, :, value_width - block:].astype(F32)
        for r in range(n_mp - 1):
            total = total + parts[c, r].astype(F32)
        value[c] = (total * inverse).astype(BF16)

        def into(blocks, r):
            return blocks.at[c, :, pl.ds(in_order.index(r) * block, block)]

        def group(r):
            return 0 if in_order.index(r) * block < near else 1

        @pl.when(finishes)
        def _():
            for r in out_order[:-1]:
                remote(value.at[c], into(gathered_own, r), value_s.at[c], own_r.at[c, group(r)],
                       mp=ring_mp[r]).start()
            pltpu.make_async_copy(value.at[c], into(gathered_own, 0), own_r.at[c, 0]).start()

        @pl.when(hands_on)
        def _():
            for r in out_order:
                remote(value.at[c], into(gathered, r), value_s.at[c], value_r.at[c, group(r)],
                       section=next_sec, mp=ring_mp[r]).start()

    def finish(c):
        @pl.when(first)
        def _():
            hidden[c] = here[c] + mixed(c, gathered_own, own_r, w_own, 1)

        @pl.when(jnp.logical_not(first))
        def _():
            hidden[c] = here[c] + mixed(c, gathered_own, own_r, w_own_t)

        @pl.when(sec < n_sec - 1)
        def _():
            remote(hidden.at[c], before.at[c], ahead_s.at[c], before_r.at[c], section=sec + 1).start()

    def within(c):
        return jnp.logical_and(c >= 0, c < chunks)

    def turn(i, carry):
        @pl.when(within(i))
        def _():
            project(i)

        @pl.when(within(i - LAG_SUM))
        def _():
            normalise(i - LAG_SUM)

        @pl.when(jnp.logical_and(finishes, within(i - LAG_OUT)))
        def _():
            finish(i - LAG_OUT)

        return carry

    lax.fori_loop(0, chunks + LAG_OUT, turn, 0)

    @pl.when(first)
    def _():
        peak_a()
        peak_b()
        peak_c()
        peak_d()

    @pl.when(jnp.logical_not(late))
    def _():
        gradient()

    def close(c, carry):
        wait_bytes(squares.at[c], square_s.at[c])
        wait_bytes(parts.at[c], part_s.at[c])

        @pl.when(finishes)
        def _():
            wait_bytes(gathered_own.at[c, :, pl.ds(0, value_width - block)], value_s.at[c])

        @pl.when(hands_on)
        def _():
            wait_bytes(gathered_own.at[c], value_s.at[c])
            wait_bytes(hidden.at[c], hidden_r.at[c])

        @pl.when(sec < n_sec - 1)
        def _():
            wait_bytes(here.at[c], ahead_s.at[c])

        @pl.when(takes_value)
        def _():
            wait_bytes(here.at[c], back_s.at[c])

        at = pl.ds(pl.multiple_of(lax.rem(c, per_micro) * rows, rows), rows)
        hidden_out[0, c // per_micro, at, :] = hidden[c]
        return carry

    lax.fori_loop(0, chunks, close, 0)
    wait_bytes(quants, quant_s)
    wait_bytes(peaks_dp, peak_s.at[0])
    wait_bytes(peaks_mp, peak_s.at[1])
    wait_bytes(peaks_opposite, peak_s.at[2])
    wait_bytes(peaks_sec, peak_s.at[3])

    @pl.when(hands_on)
    def _():
        wait_bytes(a_half, ship_s)

    @pl.when(takes_value)
    def _():
        wait_bytes(a_half, twin_s)


def solution(mesh):
    n_dp, n_sec, n_mp = (mesh.shape[a] for a in ("dp", "section", "mp"))

    def per_device(tokens, gain, w_value, w_out, grad_prev, dither):
        micro, batch, width = tokens.shape
        value_width = w_value.shape[2]
        grad_rows = grad_prev.shape[2]
        rows = CHUNK
        chunks = micro * batch // rows
        block = value_width // n_mp
        share = grad_rows // n_dp
        vmem, hbm = pl.BlockSpec(memory_space=pltpu.VMEM), pl.BlockSpec(memory_space=pl.ANY)
        dma = pltpu.SemaphoreType.DMA
        state = pltpu.VMEM((chunks, rows, width), F32)
        wide = pltpu.VMEM((chunks, rows, value_width), BF16)
        hidden, summed, scale = pl.pallas_call(
            functools.partial(kernel, (n_dp, n_sec, n_mp)),
            out_shape=(
                jax.ShapeDtypeStruct((1, micro, batch, width), F32),
                jax.ShapeDtypeStruct((1, width, share), BF16),
                jax.ShapeDtypeStruct((8, 128), F32),
            ),
            in_specs=[vmem, vmem, hbm, hbm, hbm, hbm],
            out_specs=(vmem, vmem, vmem),
            scratch_shapes=[
                pltpu.VMEM((width, value_width), BF16),
                pltpu.VMEM((width, value_width), BF16),
                pltpu.VMEM((width, value_width), BF16),
                pltpu.VMEM((value_width, width), BF16),
                pltpu.VMEM((value_width, width), BF16),
                pltpu.VMEM((width, grad_rows), BF16),
                pltpu.VMEM((width, grad_rows), BF16),
                state, state, state,
                wide,
                pltpu.VMEM((chunks, n_mp - 1, rows, block), BF16),
                pltpu.VMEM((chunks, 1, 128), F32),
                pltpu.VMEM((chunks, n_mp - 1, 1, 128), F32),
                pltpu.VMEM((chunks, rows, block), BF16),
                wide, wide,
                pltpu.VMEM((n_dp, width, share), BF16),
                pltpu.VMEM((n_dp - 1, width, share), BF16),
                pltpu.VMEM((5, 1, 128), F32),
                pltpu.VMEM((n_dp - 1, 1, 128), F32),
                pltpu.VMEM((n_mp - 1, 1, 128), F32),
                pltpu.VMEM((n_sec // 2 - 1, 1, 128), F32),
                pltpu.VMEM((1, 1, 128), F32),
                dma((4,)),
                dma((chunks,)), dma((chunks,)), dma((chunks,)), dma((chunks,)),
                dma((chunks,)), dma((chunks, 2)), dma((chunks, 2)),
                dma((chunks,)), dma((chunks,)), dma((chunks,)), dma((chunks,)),
                dma, dma, dma, dma, dma, dma,
                dma((4,)), dma((4,)),
            ],
            compiler_params=pltpu.CompilerParams(
                collective_id=0, has_side_effects=True, vmem_limit_bytes=60 * 1024 * 1024
            ),
        )(tokens, gain, w_value, jnp.swapaxes(w_out, 1, 2), jnp.swapaxes(grad_prev, 2, 3), jnp.swapaxes(dither, 2, 3))
        return hidden, jnp.swapaxes(summed, 1, 2), scale[0, 0]

    return jax.shard_map(
        per_device,
        mesh=mesh,
        in_specs=(
            P(None, "dp", "mp"),
            P("section", "mp"),
            P("section", "mp", None),
            P("section", None, "mp"),
            P("dp", "section", None, "mp"),
            P("dp", "section", None, "mp"),
        ),
        out_specs=(P("section", None, "dp", "mp"), P("section", "dp", "mp"), P()),
        check_vma=False,
    )
```
